1024 devices in a mesh: rep: 64 (over x, z_hi, core), tp: 16 (over z_lo, y).
Axes of the slice: x: 8, y: 8, z: 8 (z_hi: 4, z_lo: 2; z = z_hi * 2 + z_lo), core: 2. Of those that a mesh axis runs over, the one named last changes fastest.
Arguments:
- gradients: bfloat16 [64, 2048, 1024], P('rep', 'tp'), parts along dimension 1, may hold values from -5 to 5
- errors: float32 [64, 2048, 1024], P('rep', 'tp'), parts along dimension 1, may hold values from -0.75 to 0.75
- sign_flips: int32 [2048, 1024], P('tp'), parts along dimension 0, may hold values from -1 to 1, as said below
- first_exponents: int32 [2048], P('tp'), parts along dimension 0, may hold values from -11 to -6
- second_exponents: int32 [2048], P('tp'), parts along dimension 0, may hold values from -8 to -3
Outputs:
- err_out: float32 [64, 2048, 1024], P('rep', 'tp'), parts along dimension 1
- update: float32 [2048, 1024], P('tp'), parts along dimension 0
The draws below stay inside these ranges and needn't reach their ends.
There are 16 independent parts, one for each index of `tp`. The reference program is written for one: setup_inputs(seed, part) draws one part's arguments, and reference() takes and returns one part's arrays. A program takes and returns all parts, laid end to end along the dimension named above; each array names one. Nothing has to cross between parts.
Inputs may be any that keep to these rules, and one draw needn't show every extreme that they name: `sign_flips`: every entry is -1 or 1.
All inputs are finite; a program needn't handle non-finite values.
Results may differ from the reference program's by a relative error of at most 0.04.
Values may be sent and summed in bfloat16 or wider, within the bound.
A program may use at most 32 MiB of HBM per device.

```python
import math
import jax
import jax.numpy as jnp
from jax import lax

HB = 1024
REPS = 64
BLOCKS = 128


def draw_sign_flips(key, part):
    key = jax.random.fold_in(key, 1)
    return (2 * jax.random.randint(key, (BLOCKS, HB), 0, 2) - 1).astype(jnp.int32)


def place_ends(values, rng, smallest, top_value):
    index_at = [jax.random.randint(jax.random.fold_in(rng, axis), (), 0, length) for axis, length in enumerate(values.shape)]
    widest = values.shape.index(max(values.shape))
    beside = index_at[:widest] + [(index_at[widest] + 1) % values.shape[widest]] + index_at[widest + 1:]
    return values.at[tuple(index_at)].set(smallest).at[tuple(beside)].set(top_value)


def with_spikes(entries, own_key, source, target, parts, factor):
    owner, partner = [(jnp.arange(entries.shape[axis_at]) // (entries.shape[axis_at] // parts)).reshape([-1 if axis == axis_at else 1 for axis in range(entries.ndim)]) for axis_at in (source, target)]
    chosen = jax.random.permutation(own_key, parts)[partner]
    strong = (owner == chosen) | (owner == (partner + parts // 2) % parts)
    return jnp.where(strong, factor * entries, entries)


def block_scale(rng, shape, cuts, least, high):
    loudness, own = 1.0, jax.random.fold_in(rng, 6)
    for axis_at, shards_of in cuts:
        draws = jnp.exp(jax.random.uniform(jax.random.fold_in(own, axis_at), (shards_of,), jnp.float32, least / len(cuts), high / len(cuts)))
        loudness = loudness * jnp.repeat(draws, shape[axis_at] // shards_of).reshape([-1 if axis == axis_at else 1 for axis in range(len(shape))])
    return loudness


def centred(key, extent, spread, bound, shards=(), kind=jnp.bfloat16):
    values = jax.random.normal(key, extent, jnp.float32) * spread
    if len(shards) > 0:
        values = block_scale(key, extent, shards, -0.22, 0.18) * values
    return jnp.clip(values, min=-bound, max=bound).astype(kind)


def heavy_noise(key, shape, width, bound, shards, heavy, held_as=jnp.bfloat16):
    values = width * jax.random.normal(key, shape, jnp.float32)
    if shards:
        values = values * block_scale(key, shape, shards, -0.22, 0.18)
    return jnp.clip(with_spikes(values, jax.random.fold_in(key, 3), *heavy), -bound, bound).astype(held_as)


def setup_inputs(seed: int = 0, part: int = 0) -> dict:
    key_of = jax.random.split(jax.random.key(seed), 6)
    own_keys = jax.random.split(jax.random.fold_in(key_of[5], part), 6)
    return {
        "gradients": heavy_noise(own_keys[0], (REPS, BLOCKS, HB), 0.125, 5.0, ((0, 64),), (0, 1, 64, 4.0)),
        "errors": centred(own_keys[1], (REPS, BLOCKS, HB), 0.05, 0.75, ((0, 64),), jnp.float32),
        "sign_flips": draw_sign_flips(jax.random.fold_in(jax.random.fold_in(key_of[5], part), 71), part),
        "first_exponents": place_ends(jax.random.randint(own_keys[3], (BLOCKS,), -11, -5), jax.random.fold_in(own_keys[3], 1), -11, (-5) - 1).astype(jnp.int32),
        "second_exponents": place_ends(jax.random.randint(own_keys[4], (BLOCKS,), -8, -2), jax.random.fold_in(own_keys[4], 1), -8, (-2) - 1).astype(jnp.int32),
    }


def hadamard_matrix(length):
    positions = jnp.arange(length, dtype=jnp.int32)
    anded = positions[:, None] & positions[None, :]
    parity = jnp.zeros(anded.shape, jnp.int32)
    for bit_pos in range(length.bit_length() - 1):
        parity = parity + (anded >> bit_pos & 1)
    parity = parity & 1
    return (1 - 2 * parity).astype(jnp.float32) / math.sqrt(length)

def power_two(exponents):
    shifted = exponents.astype(jnp.int32) + 16
    result = jnp.ones(exponents.shape, jnp.float32)
    for bit_pos in range(5):
        result = result * jnp.where(shifted >> bit_pos & 1 == 1, jnp.float32(2.0 ** 2 ** bit_pos), jnp.float32(1.0))
    return result * jnp.float32(2.0 ** (-16))

def encode(values, exponents):
    scaled = values * power_two(-exponents)[..., :, None]
    return jnp.clip(scaled, -448.0, 448.0).astype(jnp.bfloat16)

def reference(gradients, errors, sign_flips, first_exponents, second_exponents):
    hadamard = hadamard_matrix(HB)
    flips = sign_flips.astype(jnp.float32)
    flipped = gradients.astype(jnp.float32) * flips[None]
    rotated = jnp.einsum('rbi,ij->rbj', flipped, hadamard, precision=lax.Precision.HIGHEST) + errors
    first_codes = encode(rotated, first_exponents)
    decoded = first_codes.astype(jnp.float32) * power_two(first_exponents)[None, :, None]
    err_out = rotated - decoded
    summed = lax.optimization_barrier(jnp.sum(decoded, axis=0))
    second_codes = encode(summed, second_exponents)
    restored = second_codes.astype(jnp.float32) * power_two(second_exponents)[:, None]
    update = flips * jnp.dot(restored, hadamard, precision=lax.Precision.HIGHEST)
    return (err_out, update)
```

```python
import jax
import jax.numpy as jnp
from jax import lax
from jax.experimental import pallas as pl
from jax.experimental.pallas import tpu as pltpu
from jax.sharding import PartitionSpec as P

LENGTH = 1024
BLOCKS = 128
HALF = 64
CHIPS = 32
ZS = 4
XS = 8
ROWS = 16
COLS = 128
FACTOR = 256
PARTS = LENGTH // FACTOR


def small_hadamard():
    i = lax.broadcasted_iota(jnp.int32, (FACTOR, FACTOR), 0)
    j = lax.broadcasted_iota(jnp.int32, (FACTOR, FACTOR), 1)
    bits = i & j
    bits = bits ^ (bits >> 4)
    bits = bits ^ (bits >> 2)
    bits = bits ^ (bits >> 1)
    return jnp.where((bits & 1) == 1, -1.0 / 32.0, 1.0 / 32.0).astype(jnp.bfloat16)


def rotate(x, matrix):
    rows = x.shape[0]
    stacked = jnp.concatenate(
        [x[:, part * FACTOR : (part + 1) * FACTOR] for part in range(PARTS)], axis=0
    )
    product = jnp.dot(stacked, matrix, preferred_element_type=jnp.float32)
    a, b, c, d = [product[part * rows : (part + 1) * rows] for part in range(PARTS)]
    ab, amb, cd, cmd = a + b, a - b, c + d, c - d
    return jnp.concatenate([ab + cd, amb + cmd, ab - cd, amb - cmd], axis=1)


def column_of(row):
    square = jnp.broadcast_to(row, (BLOCKS, BLOCKS))
    i = lax.broadcasted_iota(jnp.int32, (BLOCKS, BLOCKS), 0)
    j = lax.broadcasted_iota(jnp.int32, (BLOCKS, BLOCKS), 1)
    column = jnp.sum(jnp.where(i == j, square, 0.0), axis=1, keepdims=True)
    return jnp.broadcast_to(column, (BLOCKS, COLS))


def power_two(exponents):
    return (1 << (exponents + 16)).astype(jnp.float32) * jnp.float32(2.0**-16)


def wide(scale):
    return jnp.concatenate([scale] * (LENGTH // COLS), axis=1)


def kernel(
    g_hbm, e_hbm, f_hbm, exp1, exp2, err_hbm, upd_hbm,
    g, e, f, err, upd, codes, from_sibling, sums, parts, code2, gathered, matrix_ref,
    up1, down1, ratio, up2,
    in_sems, out_sems, core_send, core_recv, a_send, a_recv, b_send, b_recv, c_send, c_recv,
):
    me = lax.axis_index("rep")
    core = lax.rem(me, 2)
    chip = me // 2
    x, z = chip // ZS, lax.rem(chip, ZS)
    sibling = me + 1 - 2 * core

    def half(which):
        return pl.ds(pl.multiple_of(which * HALF, HALF), HALF)

    mine, other = half(core), half(1 - core)

    loads = []
    for at, rows in enumerate((other, mine)):
        for which, (source, target) in enumerate(((g_hbm.at[0], g), (f_hbm, f), (e_hbm.at[0], e))):
            copy = pltpu.make_async_copy(
                source.at[rows, :], target.at[rows, :], in_sems.at[3 * at + which]
            )
            copy.start()
            loads.append(copy)

    def peer(step):
        px = lax.rem(x + step // ZS, XS)
        pz = lax.rem(z + lax.rem(step, ZS), ZS)
        return px, pz, (px * ZS + pz) * 2 + core

    barrier = pltpu.get_barrier_semaphore()
    pl.semaphore_signal(barrier, inc=1, device_id={"rep": sibling}, device_id_type=pl.DeviceIdType.MESH)

    @pl.loop(1, CHIPS)
    def _(step):
        pl.semaphore_signal(
            barrier, inc=1, device_id={"rep": peer(step)[2]}, device_id_type=pl.DeviceIdType.MESH
        )

    s1 = power_two(exp1[...])
    s2 = power_two(exp2[...])
    up1[...] = column_of(s1)
    down1[...] = column_of(power_two(-exp1[...]))
    ratio[...] = column_of(s1 * power_two(-exp2[...]))
    up2[...] = column_of(s2)
    matrix = small_hadamard()
    matrix_ref[...] = matrix

    def first(at, rows):
        for copy in loads[3 * at : 3 * at + 3]:
            copy.wait()
        signs = f[rows, :].astype(jnp.float32)
        flipped = (g[rows, :].astype(jnp.float32) * signs).astype(jnp.bfloat16)
        rotated = rotate(flipped, matrix_ref[...]) + e[rows, :]
        code = jnp.clip(rotated * wide(down1[rows, :]), -448.0, 448.0).astype(jnp.bfloat16)
        err[rows, :] = rotated - code.astype(jnp.float32) * wide(up1[rows, :])
        codes[rows, :] = code

    stores = []

    def store(source, target, rows, sem):
        copy = pltpu.make_async_copy(source.at[rows, :], target.at[rows, :], sem)
        copy.start()
        stores.append(copy)

    first(0, other)
    pl.semaphore_wait(barrier, CHIPS)
    to_sibling = pltpu.make_async_remote_copy(
        src_ref=codes.at[other, :], dst_ref=from_sibling, send_sem=core_send, recv_sem=core_recv,
        device_id={"rep": sibling}, device_id_type=pl.DeviceIdType.MESH,
    )
    to_sibling.start()
    store(err, err_hbm.at[0], other, out_sems.at[0])
    first(1, mine)
    store(err, err_hbm.at[0], mine, out_sems.at[1])
    to_sibling.wait()
    pair = codes[mine, :].astype(jnp.float32) + from_sibling[...].astype(jnp.float32)
    sums[...] = pair.astype(jnp.bfloat16)

    def tile(px, pz, first_row):
        return (
            pl.ds(pl.multiple_of(first_row + pz * ROWS, ROWS), ROWS),
            pl.ds(pl.multiple_of(px * COLS, COLS), COLS),
        )

    @pl.loop(1, CHIPS)
    def _(step):
        px, pz, device = peer(step)
        pltpu.make_async_remote_copy(
            src_ref=sums.at[tile(px, pz, 0)], dst_ref=parts.at[step - 1],
            send_sem=a_send, recv_sem=a_recv,
            device_id={"rep": device}, device_id_type=pl.DeviceIdType.MESH,
        ).start()

    pltpu.make_async_copy(parts, parts, a_recv).wait()
    total = sums[tile(x, z, 0)].astype(jnp.float32)
    for step in range(CHIPS - 1):
        total = total + parts[step].astype(jnp.float32)
    own = tile(x, z, core * HALF)
    own_scale = ratio[own[0], :]
    second = jnp.clip(total * own_scale, -448.0, 448.0).astype(jnp.bfloat16)
    gathered[own] = second

    @pl.loop(1, CHIPS)
    def _(step):
        device = peer(step)[2]
        pltpu.make_async_remote_copy(
            src_ref=gathered.at[own], dst_ref=gathered.at[own],
            send_sem=b_send, recv_sem=b_recv,
            device_id={"rep": device}, device_id_type=pl.DeviceIdType.MESH,
        ).start()

    def last(rows):
        restored = rotate(gathered[rows, :], matrix_ref[...])
        upd[rows, :] = restored * wide(up2[rows, :]) * f[rows, :].astype(jnp.float32)

    pltpu.make_async_copy(parts, parts, b_recv).wait()
    forward = pltpu.make_async_remote_copy(
        src_ref=gathered.at[mine, :], dst_ref=gathered.at[mine, :], send_sem=c_send, recv_sem=c_recv,
        device_id={"rep": sibling}, device_id_type=pl.DeviceIdType.MESH,
    )
    forward.start()
    last(mine)
    store(upd, upd_hbm, mine, out_sems.at[2])
    forward.wait()
    last(other)
    store(upd, upd_hbm, other, out_sems.at[3])
    pltpu.make_async_copy(parts, parts, a_send).wait()
    pltpu.make_async_copy(parts, parts, b_send).wait()
    for copy in stores:
        copy.wait()


def per_device(gradients, errors, sign_flips, first_exponents, second_exponents):
    any_space = pl.BlockSpec(memory_space=pl.ANY)
    vmem = pl.BlockSpec(memory_space=pltpu.VMEM)
    whole = (BLOCKS, LENGTH)
    f32, bf16 = jnp.float32, jnp.bfloat16
    dma = pltpu.SemaphoreType.DMA
    return pl.pallas_call(
        kernel,
        out_shape=(jax.ShapeDtypeStruct((1, *whole), f32), jax.ShapeDtypeStruct(whole, f32)),
        in_specs=[any_space, any_space, any_space, vmem, vmem],
        out_specs=(any_space, any_space),
        scratch_shapes=[
            pltpu.VMEM(whole, bf16), pltpu.VMEM(whole, f32), pltpu.VMEM(whole, jnp.int32),
            pltpu.VMEM(whole, f32), pltpu.VMEM(whole, f32),
            pltpu.VMEM(whole, bf16), pltpu.VMEM((HALF, LENGTH), bf16), pltpu.VMEM((HALF, LENGTH), bf16),
            pltpu.VMEM((CHIPS - 1, ROWS, COLS), bf16), pltpu.VMEM((ROWS, COLS), bf16),
            pltpu.VMEM(whole, bf16), pltpu.VMEM((FACTOR, FACTOR), bf16),
            pltpu.VMEM((BLOCKS, COLS), f32), pltpu.VMEM((BLOCKS, COLS), f32),
            pltpu.VMEM((BLOCKS, COLS), f32), pltpu.VMEM((BLOCKS, COLS), f32),
            dma((6,)), dma((4,)), dma, dma, dma, dma, dma, dma, dma, dma,
        ],
        compiler_params=pltpu.CompilerParams(
            collective_id=0, has_side_effects=True, vmem_limit_bytes=60 * 2**20
        ),
    )(
        gradients, errors, sign_flips,
        first_exponents.reshape(1, BLOCKS), second_exponents.reshape(1, BLOCKS),
    )


def solution(mesh):
    in_specs = (P("rep", "tp", None), P("rep", "tp", None), P("tp", None), P("tp"), P("tp"))
    out_specs = (P("rep", "tp", None), P("tp", None))
    return jax.shard_map(
        per_device, mesh=mesh, in_specs=in_specs, out_specs=out_specs, check_vma=False
    )
```

```python
import jax
import jax.numpy as jnp
from jax import lax
from jax.experimental import pallas as pl
from jax.experimental.pallas import tpu as pltpu
from jax.sharding import PartitionSpec as P

LENGTH = 1024
BLOCKS = 128
HALF = 64
XS = 8
ZS = 4
ROWS = 16
COLS = 512
LANES = 128
FACTOR = 256
PARTS = LENGTH // FACTOR
MESH = pl.DeviceIdType.MESH
FAR_FIRST = (4, 3, 5, 2, 6, 1, 7)
NEAR_FIRST = (1, 7, 2, 6, 3, 5, 4)


def small_hadamard():
    i = lax.broadcasted_iota(jnp.int32, (FACTOR, FACTOR), 0)
    j = lax.broadcasted_iota(jnp.int32, (FACTOR, FACTOR), 1)
    bits = i & j
    bits = bits ^ (bits >> 4)
    bits = bits ^ (bits >> 2)
    bits = bits ^ (bits >> 1)
    return jnp.where((bits & 1) == 1, -1.0 / 32.0, 1.0 / 32.0).astype(jnp.bfloat16)


def rotate(x, matrix):
    rows = x.shape[0]
    stacked = jnp.concatenate(
        [x[:, part * FACTOR : (part + 1) * FACTOR] for part in range(PARTS)], axis=0
    )
    product = jnp.dot(stacked, matrix, preferred_element_type=jnp.float32)
    a, b, c, d = [product[part * rows : (part + 1) * rows] for part in range(PARTS)]
    ab, amb, cd, cmd = a + b, a - b, c + d, c - d
    return jnp.concatenate([ab + cd, amb + cmd, ab - cd, amb - cmd], axis=1)


def column_of(row):
    square = jnp.broadcast_to(row, (BLOCKS, BLOCKS))
    i = lax.broadcasted_iota(jnp.int32, (BLOCKS, BLOCKS), 0)
    j = lax.broadcasted_iota(jnp.int32, (BLOCKS, BLOCKS), 1)
    column = jnp.sum(jnp.where(i == j, square, 0.0), axis=1, keepdims=True)
    return jnp.broadcast_to(column, (BLOCKS, LANES))


def power_two(exponents):
    return (1 << (exponents + 16)).astype(jnp.float32) * jnp.float32(2.0**-16)


def wide(scale, columns):
    return jnp.concatenate([scale] * (columns // LANES), axis=1)


def reduce_kernel(
    g_hbm, e_hbm, f_hbm, exp1_hbm, exp2_hbm, gathered, err, f, matrix, up2,
    g, e, codes, from_sibling, sums, parts, exp1, exp2, up1, down1, ratio,
    exp_sems, in_sems, pair_send, pair_recv, a_send, a_recv, z_send, z_recv, x_send, x_recv, c_send, c_recv,
):
    me = lax.axis_index("rep")
    core = lax.rem(me, 2)
    chip = me // 2
    x, z = chip // ZS, lax.rem(chip, ZS)
    sibling = me + 1 - 2 * core

    def device(px, pz):
        return {"rep": (px * ZS + pz) * 2 + core}

    def turned(step):
        return lax.rem(x + step, XS)

    def half(which):
        return pl.ds(pl.multiple_of(which * HALF, HALF), HALF)

    mine, other = half(core), half(1 - core)

    def slab(px, first_row):
        return (
            pl.ds(pl.multiple_of(first_row + (px // 2) * ROWS, ROWS), ROWS),
            pl.ds(pl.multiple_of(lax.rem(px, 2) * COLS, COLS), COLS),
        )

    small_loads = [
        pltpu.make_async_copy(exp1_hbm, exp1, exp_sems.at[0]),
        pltpu.make_async_copy(exp2_hbm, exp2, exp_sems.at[1]),
    ]
    for copy in small_loads:
        copy.start()
    loads = []
    for at, rows in enumerate((other, mine)):
        for which, (source, target) in enumerate(((g_hbm.at[0], g), (f_hbm, f), (e_hbm.at[0], e))):
            copy = pltpu.make_async_copy(
                source.at[rows, :], target.at[rows, :], in_sems.at[3 * at + which]
            )
            copy.start()
            loads.append(copy)

    barrier = pltpu.get_barrier_semaphore()
    pl.semaphore_signal(barrier, inc=1, device_id={"rep": sibling}, device_id_type=MESH)

    @pl.when(z == 0)
    def _():
        @pl.loop(1, XS * ZS)
        def _(step):
            pl.semaphore_signal(
                barrier, inc=1,
                device_id=device(turned(lax.rem(step, XS)), lax.rem(z + step // XS, ZS)),
                device_id_type=MESH,
            )

    matrix[...] = small_hadamard()
    for copy in small_loads:
        copy.wait()
    s1 = power_two(exp1[...])
    up1[...] = column_of(s1)
    down1[...] = column_of(power_two(-exp1[...]))
    ratio[...] = column_of(s1 * power_two(-exp2[...]))
    up2[...] = column_of(power_two(exp2[...]))

    def first(at, rows):
        for copy in loads[3 * at : 3 * at + 3]:
            copy.wait()
        signs = f[rows, :].astype(jnp.float32)
        flipped = (g[rows, :].astype(jnp.float32) * signs).astype(jnp.bfloat16)
        rotated = rotate(flipped, matrix[...]) + e[rows, :]
        code = jnp.clip(rotated * wide(down1[rows, :], LENGTH), -448.0, 448.0).astype(jnp.bfloat16)
        err[rows, :] = rotated - code.astype(jnp.float32) * wide(up1[rows, :], LENGTH)
        codes[rows, :] = code

    first(0, other)
    pl.semaphore_wait(barrier, jnp.where(z == 0, XS, XS + 1))
    to_sibling = pltpu.make_async_remote_copy(
        src_ref=codes.at[other, :], dst_ref=from_sibling, send_sem=pair_send, recv_sem=pair_recv,
        device_id={"rep": sibling}, device_id_type=MESH,
    )
    to_sibling.start()
    first(1, mine)
    to_sibling.wait()
    pair = codes[mine, :].astype(jnp.float32) + from_sibling[...].astype(jnp.float32)
    sums[...] = pair.astype(jnp.bfloat16)

    def to_owner(px):
        pltpu.make_async_remote_copy(
            src_ref=sums.at[slab(px, 0)], dst_ref=parts.at[z, x],
            send_sem=a_send, recv_sem=a_recv.at[z],
            device_id=device(px, 0), device_id_type=MESH,
        ).start()

    for step in FAR_FIRST:
        to_owner(turned(step))

    @pl.when(z != 0)
    def _():
        to_owner(x)

    own = slab(x, core * HALF)

    def to_relay(pz):
        pltpu.make_async_remote_copy(
            src_ref=gathered.at[own], dst_ref=gathered.at[own],
            send_sem=z_send, recv_sem=z_recv,
            device_id=device(x, pz), device_id_type=MESH,
        ).start()

    def to_row(px):
        pltpu.make_async_remote_copy(
            src_ref=gathered.at[own], dst_ref=gathered.at[own],
            send_sem=x_send, recv_sem=x_recv.at[x],
            device_id=device(px, z), device_id_type=MESH,
        ).start()

    @pl.when(z == 0)
    def _():
        parts[0, x] = sums[slab(x, 0)]
        total = jnp.zeros((ROWS, COLS), jnp.float32)
        for plane in range(ZS):
            landed = parts.at[plane] if plane else parts.at[0, pl.ds(0, XS - 1)]
            pltpu.make_async_copy(landed, landed, a_recv.at[plane]).wait()
            for column in range(XS):
                total = total + parts[plane, column].astype(jnp.float32)
        scaled = total * wide(ratio[own[0], :], COLS)
        gathered[own] = jnp.clip(scaled, -448.0, 448.0).astype(jnp.bfloat16)
        to_relay(1)
        for step in FAR_FIRST:
            to_row(turned(step))
        to_relay(2)
        to_relay(3)

    @pl.when(z != 0)
    def _():
        pltpu.make_async_copy(gathered.at[own], gathered.at[own], z_recv).wait()
        for step in FAR_FIRST:
            to_row(turned(step))

    def to_other_core(px):
        rows = slab(px, core * HALF)
        pltpu.make_async_remote_copy(
            src_ref=gathered.at[rows], dst_ref=gathered.at[rows],
            send_sem=c_send, recv_sem=c_recv,
            device_id={"rep": sibling}, device_id_type=MESH,
        ).start()

    to_other_core(x)
    for step in NEAR_FIRST:
        px = turned(step)
        rows = slab(px, core * HALF)
        pltpu.make_async_copy(gathered.at[rows], gathered.at[rows], x_recv.at[px]).wait()
        to_other_core(px)

    seven = parts.at[0, pl.ds(0, XS - 1)]
    pltpu.make_async_copy(seven, seven, x_send).wait()
    pltpu.make_async_copy(parts.at[0], parts.at[0], c_send).wait()

    @pl.when(z == 0)
    def _():
        three = parts.at[0, pl.ds(0, ZS - 1)]
        pltpu.make_async_copy(seven, seven, a_send).wait()
        pltpu.make_async_copy(three, three, z_send).wait()

    @pl.when(z != 0)
    def _():
        pltpu.make_async_copy(parts.at[0], parts.at[0], a_send).wait()

    pltpu.make_async_copy(parts.at[0], parts.at[0], c_recv).wait()


def update_kernel(gathered, err, f, matrix, up2, err_hbm, upd_hbm, upd, out_sems):
    stores = [pltpu.make_async_copy(err, err_hbm.at[0], out_sems.at[0])]
    stores[0].start()
    for at in range(2):
        rows = pl.ds(at * HALF, HALF)
        restored = rotate(gathered[rows, :], matrix[...]) * wide(up2[rows, :], LENGTH)
        upd[rows, :] = restored * f[rows, :].astype(jnp.float32)
        stores.append(
            pltpu.make_async_copy(upd.at[rows, :], upd_hbm.at[rows, :], out_sems.at[1 + at])
        )
        stores[-1].start()
    for copy in stores:
        copy.wait()


def per_device(gradients, errors, sign_flips, first_exponents, second_exponents):
    hbm = pl.BlockSpec(memory_space=pl.ANY)
    vmem = pl.BlockSpec(memory_space=pltpu.VMEM)
    whole = (BLOCKS, LENGTH)
    f32, bf16, i32 = jnp.float32, jnp.bfloat16, jnp.int32
    dma = pltpu.SemaphoreType.DMA
    arguments = (
        gradients, errors, sign_flips,
        first_exponents.reshape(1, BLOCKS), second_exponents.reshape(1, BLOCKS),
    )
    held = pl.pallas_call(
        reduce_kernel,
        out_shape=(
            pltpu.VMEM(whole, bf16), pltpu.VMEM(whole, f32), pltpu.VMEM(whole, i32),
            pltpu.VMEM((FACTOR, FACTOR), bf16), pltpu.VMEM((BLOCKS, LANES), f32),
        ),
        in_specs=[hbm] * 5,
        out_specs=(vmem,) * 5,
        scratch_shapes=[
            pltpu.VMEM(whole, bf16), pltpu.VMEM(whole, f32),
            pltpu.VMEM(whole, bf16), pltpu.VMEM((HALF, LENGTH), bf16), pltpu.VMEM((HALF, LENGTH), bf16),
            pltpu.VMEM((ZS, XS, ROWS, COLS), bf16),
            pltpu.VMEM((1, BLOCKS), i32), pltpu.VMEM((1, BLOCKS), i32),
            pltpu.VMEM((BLOCKS, LANES), f32), pltpu.VMEM((BLOCKS, LANES), f32),
            pltpu.VMEM((BLOCKS, LANES), f32),
            dma((2,)), dma((6,)), dma, dma, dma, dma((ZS,)), dma, dma, dma, dma((XS,)), dma, dma,
        ],
        compiler_params=pltpu.CompilerParams(
            collective_id=0, has_side_effects=True, vmem_limit_bytes=16 * 2**20
        ),
    )(*[pltpu.with_memory_space_constraint(array, pltpu.HBM) for array in arguments])
    return pl.pallas_call(
        update_kernel,
        out_shape=(jax.ShapeDtypeStruct((1, *whole), f32), jax.ShapeDtypeStruct(whole, f32)),
        in_specs=[vmem] * 5,
        out_specs=(hbm, hbm),
        scratch_shapes=[pltpu.VMEM(whole, f32), dma((3,))],
        compiler_params=pltpu.CompilerParams(vmem_limit_bytes=16 * 2**20),
    )(*held)


def solution(mesh):
    in_specs = (P("rep", "tp", None), P("rep", "tp", None), P("tp", None), P("tp"), P("tp"))
    out_specs = (P("rep", "tp", None), P("tp", None))
    return jax.shard_map(
        per_device, mesh=mesh, in_specs=in_specs, out_specs=out_specs, check_vma=False
    )
```

```python
import jax
import jax.numpy as jnp
from jax import lax
from jax.experimental import pallas as pl
from jax.experimental.pallas import tpu as pltpu
from jax.sharding import PartitionSpec as P

LENGTH = 1024
BLOCKS = 128
HALF = 64
XS = 8
ZS = 4
ROWS = 16
COLS = 512
LANES = 128
FACTOR = 256
PARTS = LENGTH // FACTOR
MESH = pl.DeviceIdType.MESH
CHUNK = 32
CHUNK_SLABS = ((0, 1, 5, 4), (7, 2, 6, 3))
EARLY_FIRST = (0, 1, 7, 2, 6, 3, 5, 4)
NEAR_FIRST = (0, 1, 7, 2, 6, 3, 5, 4)


def small_hadamard():
    i = lax.broadcasted_iota(jnp.int32, (FACTOR, FACTOR), 0)
    j = lax.broadcasted_iota(jnp.int32, (FACTOR, FACTOR), 1)
    bits = i & j
    bits = bits ^ (bits >> 4)
    bits = bits ^ (bits >> 2)
    bits = bits ^ (bits >> 1)
    return jnp.where((bits & 1) == 1, -1.0 / 32.0, 1.0 / 32.0).astype(jnp.bfloat16)


def rotate(x, matrix):
    rows = x.shape[0]
    stacked = jnp.concatenate(
        [x[:, part * FACTOR : (part + 1) * FACTOR] for part in range(PARTS)], axis=0
    )
    product = jnp.dot(stacked, matrix, preferred_element_type=jnp.float32)
    a, b, c, d = [product[part * rows : (part + 1) * rows] for part in range(PARTS)]
    ab, amb, cd, cmd = a + b, a - b, c + d, c - d
    return jnp.concatenate([ab + cd, amb + cmd, ab - cd, amb - cmd], axis=1)


def columns_of(row1, row2):
    both = jnp.broadcast_to((row1 + 64 * row2).astype(jnp.float32), (BLOCKS, BLOCKS))
    i = lax.broadcasted_iota(jnp.int32, (BLOCKS, BLOCKS), 0)
    j = lax.broadcasted_iota(jnp.int32, (BLOCKS, BLOCKS), 1)
    column = jnp.sum(jnp.where(i == j, both, 0.0), axis=1, keepdims=True)
    packed = jnp.broadcast_to(column, (BLOCKS, LANES)).astype(jnp.int32)
    second = (packed + 32) >> 6
    return packed - 64 * second, second


def power_two(exponents):
    return (1 << (exponents + 16)).astype(jnp.float32) * jnp.float32(2.0**-16)


def wide(scale, columns):
    return jnp.concatenate([scale] * (columns // LANES), axis=1)


def reduce_kernel(
    g_hbm, e_hbm, f_hbm, exp1_hbm, exp2_hbm, err, upd,
    g, e, f, codes, from_sibling, sums, parts, passed, gathered, matrix, exp1, exp2, up1, down1, ratio, up2,
    exp_sems, in_sems, pair_send, pair_recv, a_send, a_recv, p_send, x_send, x_recv, c_send, c_recv,
):
    me = lax.axis_index("rep")
    core = lax.rem(me, 2)
    chip = me // 2
    x, z = chip // ZS, lax.rem(chip, ZS)
    sibling = me + 1 - 2 * core
    moved = lax.axis_index("tp") == 0
    late = moved & (x == 0) & (z == 0) & (core == 0)
    owns = (z == 0) & jnp.logical_not(late)
    owns_more = moved & (x == 0) & (z == 0) & (core == 1)
    elsewhere = moved & (core == 0)

    def device(px, pz, at_core=core):
        return {"rep": (px * ZS + pz) * 2 + at_core}

    def rows_at(first_row, count):
        return pl.ds(pl.multiple_of(first_row, ROWS), count)

    def slab(s, first_row):
        return (
            rows_at(first_row + lax.rem(s, XS // 2) * ROWS, ROWS),
            pl.ds(pl.multiple_of((s // (XS // 2)) * COLS, COLS), COLS),
        )

    mine, other = core * HALF, (1 - core) * HALF

    small_loads = [
        pltpu.make_async_copy(exp1_hbm, exp1, exp_sems.at[0]),
        pltpu.make_async_copy(exp2_hbm, exp2, exp_sems.at[1]),
    ]
    for copy in small_loads:
        copy.start()
    loads = {}
    for at, (base, chunk) in enumerate(((other, 0), (other, 1), (mine, 0), (mine, 1))):
        rows = rows_at(base + chunk * CHUNK, CHUNK)
        for which, (source, target) in enumerate(((g_hbm.at[0], g), (f_hbm, f), (e_hbm.at[0], e))):
            copy = pltpu.make_async_copy(
                source.at[rows, :], target.at[rows, :], in_sems.at[3 * at + which]
            )
            copy.start()
            loads[at, which] = copy

    barrier = pltpu.get_barrier_semaphore()
    pl.semaphore_signal(barrier, inc=1, device_id={"rep": sibling}, device_id_type=MESH)

    def greet(at_core):
        @pl.loop(1, XS)
        def _(step):
            pl.semaphore_signal(
                barrier, inc=1, device_id=device(lax.rem(x + step, XS), 0, at_core),
                device_id_type=MESH,
            )

        @pl.loop(0, 2 * XS)
        def _(step):
            pl.semaphore_signal(
                barrier, inc=1, device_id=device(lax.rem(x + step // 2, XS), 1 + 2 * lax.rem(step, 2), at_core),
                device_id_type=MESH,
            )

    pl.when(owns)(lambda: greet(core))
    pl.when(owns_more)(lambda: greet(0))

    @pl.when(z == 1)
    def _():
        @pl.loop(0, XS)
        def _(step):
            pl.semaphore_signal(
                barrier, inc=1, device_id=device(lax.rem(x + step, XS), 2), device_id_type=MESH
            )

    matrix[...] = small_hadamard()
    for copy in small_loads:
        copy.wait()
    exponent1, exponent2 = columns_of(exp1[...], exp2[...])
    scale1 = power_two(exponent1)
    up1[...] = scale1
    down1[...] = power_two(-exponent1)

    def first(at, first_row):
        rows = rows_at(first_row, CHUNK)
        for which in range(3):
            loads[at, which].wait()
        signs = f[rows, :].astype(jnp.float32)
        flipped = (g[rows, :].astype(jnp.float32) * signs).astype(jnp.bfloat16)
        rotated = rotate(flipped, matrix[...]) + e[rows, :]
        code = jnp.clip(rotated * wide(down1[rows, :], LENGTH), -448.0, 448.0).astype(jnp.bfloat16)
        err[rows, :] = rotated - code.astype(jnp.float32) * wide(up1[rows, :], LENGTH)
        codes[rows, :] = code

    to_sibling = []
    for chunk in range(2):
        first(chunk, other + chunk * CHUNK)
        if chunk == 0:
            pl.semaphore_wait(barrier, jnp.where(z == 0, XS, XS + 1))
        to_sibling.append(pltpu.make_async_remote_copy(
            src_ref=codes.at[rows_at(other + chunk * CHUNK, CHUNK), :],
            dst_ref=from_sibling.at[pl.ds(chunk * CHUNK, CHUNK), :],
            send_sem=pair_send.at[chunk], recv_sem=pair_recv.at[chunk],
            device_id={"rep": sibling}, device_id_type=MESH,
        ))
        to_sibling[-1].start()
    for chunk in range(2):
        first(2 + chunk, mine + chunk * CHUNK)

    def to_owner(s):
        away = (elsewhere & (s == 0)).astype(jnp.int32)
        buffer = jnp.where(z == 2, 0, away)
        pltpu.make_async_remote_copy(
            src_ref=sums.at[slab(s, 0)], dst_ref=parts.at[buffer, z, x],
            send_sem=a_send, recv_sem=a_recv.at[buffer, z],
            device_id=device(s, jnp.where(z == 2, 1, 0), core + buffer), device_id_type=MESH,
        ).start()

    for chunk in range(2):
        to_sibling[chunk].wait()
        rows = pl.ds(chunk * CHUNK, CHUNK)
        pair = codes[rows_at(mine + chunk * CHUNK, CHUNK), :].astype(jnp.float32)
        sums[rows, :] = (pair + from_sibling[rows, :].astype(jnp.float32)).astype(jnp.bfloat16)
        for s in CHUNK_SLABS[chunk]:
            pl.when(jnp.logical_not(owns & (x == s)))(lambda s=s: to_owner(s))

    ratio[...] = scale1 * power_two(-exponent2)
    up2[...] = power_two(exponent2)

    def plane_sum(total, buffer, plane, count):
        for column in range(count):
            total = total + parts[buffer, plane, column].astype(jnp.float32)
        return total

    def slots(count):
        return parts.at[0, 0, pl.ds(0, count)]

    def wait_for(landed, sem):
        pltpu.make_async_copy(landed, landed, sem).wait()

    @pl.when(z == 1)
    def _():
        wait_for(parts.at[0, 2], a_recv.at[0, 2])
        total = plane_sum(jnp.zeros((ROWS, COLS), jnp.float32), 0, 2, XS)
        passed[...] = total.astype(jnp.bfloat16)
        buffer = (elsewhere & (x == 0)).astype(jnp.int32)
        pltpu.make_async_remote_copy(
            src_ref=passed, dst_ref=parts.at[buffer, 2, 0],
            send_sem=p_send, recv_sem=a_recv.at[buffer, 2],
            device_id=device(x, 0, core + buffer), device_id_type=MESH,
        ).start()

    def send_slab(s, at, device_id):
        own = slab(s, at)
        pltpu.make_async_remote_copy(
            src_ref=gathered.at[own], dst_ref=gathered.at[own],
            send_sem=x_send, recv_sem=x_recv.at[s],
            device_id=device_id, device_id_type=MESH,
        ).start()

    def to_row(s):
        for px in EARLY_FIRST:
            pl.when(px != x)(lambda px=px: send_slab(s, mine, device(px, z)))

    def own_slab(s, buffer, at):
        own = slab(s, at)
        total = jnp.zeros((ROWS, COLS), jnp.float32)
        for plane in range(ZS):
            if plane == 0:
                wait_for(slots(XS - 1 + buffer), a_recv.at[buffer, 0])
            elif plane == 2:
                wait_for(slots(1), a_recv.at[buffer, 2])
            else:
                wait_for(slots(XS), a_recv.at[buffer, plane])
            total = plane_sum(total, buffer, plane, 1 if plane == 2 else XS)
        scaled = total * wide(ratio[own[0], :], COLS)
        gathered[own] = jnp.clip(scaled, -448.0, 448.0).astype(jnp.bfloat16)

    def wait_slab(s):
        own = slab(s, mine)
        pltpu.make_async_copy(gathered.at[own], gathered.at[own], x_recv.at[s]).wait()

    def to_other_core(s):
        own = slab(s, mine)
        pltpu.make_async_remote_copy(
            src_ref=gathered.at[own], dst_ref=gathered.at[own],
            send_sem=c_send, recv_sem=c_recv.at[s],
            device_id={"rep": sibling}, device_id_type=MESH,
        ).start()

    @pl.when(owns)
    def _():
        parts[0, 0, x] = sums[slab(x, 0)]
        own_slab(x, 0, mine)
        send_slab(x, mine, device(x, 1))
        to_row(x)
        send_slab(x, mine, device(x, 2))
        send_slab(x, mine, device(x, 3))

    @pl.when(owns_more)
    def _():
        own_slab(0, 1, 0)
        send_slab(0, 0, device(0, 1, 0))
        for px in EARLY_FIRST:
            send_slab(0, 0, device(px, 0, 0))
        send_slab(0, 0, device(0, 2, 0))
        send_slab(0, 0, device(0, 3, 0))

    @pl.when(z != 0)
    def _():
        wait_slab(x)
        to_row(x)

    for step in NEAR_FIRST:
        s = lax.rem(x + step, XS)
        if step == 0:
            pl.when(late)(lambda: wait_slab(x))
            pl.when(jnp.logical_not(late))(lambda: to_other_core(x))
        else:
            wait_slab(s)
            to_other_core(s)

    def last(rows):
        restored = rotate(gathered[rows, :], matrix[...]) * wide(up2[rows, :], LENGTH)
        upd[rows, :] = restored * f[rows, :].astype(jnp.float32)

    last(rows_at(mine, HALF))
    for group in range(XS // 2):
        for s in (group, group + XS // 2):
            held = owns_more & (s == 0)
            pl.when(jnp.logical_not(held))(lambda s=s: wait_for(slots(1), c_recv.at[s]))
        last(rows_at(other + group * ROWS, ROWS))

    @pl.when(owns)
    def _():
        wait_for(slots(XS - 1), a_send)
        wait_for(parts.at[0, pl.ds(0, 2), pl.ds(0, 5)], x_send)

    @pl.when(owns_more)
    def _():
        wait_for(slots(XS), x_send)
        wait_for(slots(3), x_send)

    @pl.when(jnp.logical_not(owns))
    def _():
        wait_for(slots(XS), a_send)

    @pl.when(z != 0)
    def _():
        wait_for(slots(XS - 1), x_send)

    @pl.when(z == 1)
    def _():
        wait_for(passed, p_send)

    wait_for(slots(XS - 1), c_send)
    pl.when(jnp.logical_not(late))(lambda: wait_for(slots(1), c_send))


def write_kernel(err, upd, err_hbm, upd_hbm, out_sems):
    stores = []
    for at in range(BLOCKS // CHUNK):
        rows = pl.ds(at * CHUNK, CHUNK)
        for which, (source, target) in enumerate(((err, err_hbm.at[0]), (upd, upd_hbm))):
            copy = pltpu.make_async_copy(
                source.at[rows, :], target.at[rows, :], out_sems.at[2 * at + which]
            )
            copy.start()
            stores.append(copy)
    for copy in stores:
        copy.wait()


def per_device(gradients, errors, sign_flips, first_exponents, second_exponents):
    hbm = pl.BlockSpec(memory_space=pl.ANY)
    vmem = pl.BlockSpec(memory_space=pltpu.VMEM)
    whole = (BLOCKS, LENGTH)
    f32, bf16, i32 = jnp.float32, jnp.bfloat16, jnp.int32
    dma = pltpu.SemaphoreType.DMA
    scale = pltpu.VMEM((BLOCKS, LANES), f32)
    arguments = (
        gradients, errors, sign_flips,
        first_exponents.reshape(1, BLOCKS), second_exponents.reshape(1, BLOCKS),
    )
    held = pl.pallas_call(
        reduce_kernel,
        out_shape=(pltpu.VMEM(whole, f32), pltpu.VMEM(whole, f32)),
        in_specs=[hbm] * 5,
        out_specs=(vmem, vmem),
        scratch_shapes=[
            pltpu.VMEM(whole, bf16), pltpu.VMEM(whole, f32), pltpu.VMEM(whole, i32),
            pltpu.VMEM(whole, bf16), pltpu.VMEM((HALF, LENGTH), bf16), pltpu.VMEM((HALF, LENGTH), bf16),
            pltpu.VMEM((2, ZS, XS, ROWS, COLS), bf16), pltpu.VMEM((ROWS, COLS), bf16),
            pltpu.VMEM(whole, bf16),
            pltpu.VMEM((FACTOR, FACTOR), bf16),
            pltpu.VMEM((1, BLOCKS), i32), pltpu.VMEM((1, BLOCKS), i32), scale, scale, scale, scale,
            dma((2,)), dma((12,)), dma((2,)), dma((2,)), dma, dma((2, ZS)), dma, dma, dma((XS,)),
            dma, dma((XS,)),
        ],
        compiler_params=pltpu.CompilerParams(
            collective_id=0, has_side_effects=True, vmem_limit_bytes=16 * 2**20
        ),
    )(*[pltpu.with_memory_space_constraint(array, pltpu.HBM) for array in arguments])
    return pl.pallas_call(
        write_kernel,
        out_shape=(jax.ShapeDtypeStruct((1, *whole), f32), jax.ShapeDtypeStruct(whole, f32)),
        in_specs=[vmem, vmem],
        out_specs=(hbm, hbm),
        scratch_shapes=[dma((2 * BLOCKS // CHUNK,))],
        compiler_params=pltpu.CompilerParams(vmem_limit_bytes=16 * 2**20),
    )(*held)


def solution(mesh):
    in_specs = (P("rep", "tp", None), P("rep", "tp", None), P("tp", None), P("tp"), P("tp"))
    out_specs = (P("rep", "tp", None), P("tp", None))
    return jax.shard_map(
        per_device, mesh=mesh, in_specs=in_specs, out_specs=out_specs, check_vma=False
    )
```

```python
import jax
import jax.numpy as jnp
from jax import lax
from jax.experimental import pallas as pl
from jax.experimental.pallas import tpu as pltpu
from jax.sharding import PartitionSpec as P

LENGTH = 1024
BLOCKS = 128
HALF = 64
XS = 8
ZS = 4
ROWS = 16
UNIT = 256
COLS = 768
LANES = 128
FACTOR = 256
PARTS = LENGTH // FACTOR
MESH = pl.DeviceIdType.MESH
CHUNK = 32
CHUNK_SLABS = ((4, 0, 3, 5), (2, 6, 1, 7))
SLABS = (
    (0, 0, 768), (48, 0, 512), (32, 0, 512), (16, 0, 512),
    (0, 768, 256), (16, 512, 512), (32, 512, 512), (48, 512, 512),
)
WIDTHS = (256, 512, 768)
EARLY_FIRST = (0, 1, 7, 2, 6, 3, 5, 4)
PAIRS = XS // 2


def small_hadamard():
    i = lax.broadcasted_iota(jnp.int32, (FACTOR, FACTOR), 0)
    j = lax.broadcasted_iota(jnp.int32, (FACTOR, FACTOR), 1)
    bits = i & j
    bits = bits ^ (bits >> 4)
    bits = bits ^ (bits >> 2)
    bits = bits ^ (bits >> 1)
    return jnp.where((bits & 1) == 1, -1.0 / 32.0, 1.0 / 32.0).astype(jnp.bfloat16)


def rotate(x, matrix):
    rows = x.shape[0]
    stacked = jnp.concatenate(
        [x[:, part * FACTOR : (part + 1) * FACTOR] for part in range(PARTS)], axis=0
    )
    product = jnp.dot(stacked, matrix, preferred_element_type=jnp.float32)
    a, b, c, d = [product[part * rows : (part + 1) * rows] for part in range(PARTS)]
    ab, amb, cd, cmd = a + b, a - b, c + d, c - d
    return jnp.concatenate([ab + cd, amb + cmd, ab - cd, amb - cmd], axis=1)


def columns_of(row1, row2):
    both = jnp.broadcast_to((row1 + 64 * row2).astype(jnp.float32), (BLOCKS, BLOCKS))
    i = lax.broadcasted_iota(jnp.int32, (BLOCKS, BLOCKS), 0)
    j = lax.broadcasted_iota(jnp.int32, (BLOCKS, BLOCKS), 1)
    column = jnp.sum(jnp.where(i == j, both, 0.0), axis=1, keepdims=True)
    packed = jnp.broadcast_to(column, (BLOCKS, LANES)).astype(jnp.int32)
    second = (packed + 32) >> 6
    return packed - 64 * second, second


def power_two(exponents):
    return (1 << (exponents + 16)).astype(jnp.float32) * jnp.float32(2.0**-16)


def wide(scale, columns):
    return jnp.concatenate([scale] * (columns // LANES), axis=1)


def reduce_kernel(
    g_hbm, e_hbm, f_hbm, exp1_hbm, exp2_hbm, err, upd,
    g, e, f, codes, from_sibling, sums, parts, passed, gathered, matrix, exp1, exp2, up1, down1, ratio, up2,
    exp_sems, in_sems, pair_send, pair_recv, a_send, a_recv, p_send, x_send, x_recv, c_send, c_recv,
):
    me = lax.axis_index("rep")
    core = lax.rem(me, 2)
    chip = me // 2
    x, z = chip // ZS, lax.rem(chip, ZS)
    sibling = me + 1 - 2 * core
    moved = lax.axis_index("tp") == 0
    late = moved & (x == 0) & (z == 0) & (core == 0)
    owns = (z == 0) & jnp.logical_not(late)
    owns_more = moved & (x == 0) & (z == 0) & (core == 1)
    elsewhere = moved & (core == 0)

    def device(px, pz, at_core=core):
        return {"rep": (px * ZS + pz) * 2 + at_core}

    def rows_at(first_row, count):
        return pl.ds(pl.multiple_of(first_row, ROWS), count)

    def slab(s, first_row):
        if isinstance(s, int):
            row, column, width = SLABS[s]
            return rows_at(first_row + row, ROWS), pl.ds(column, width)
        index, width = s
        row, column = jnp.int32(0), jnp.int32(0)
        for at, (own_row, own_column, own_width) in enumerate(SLABS):
            if own_width == width:
                row = jnp.where(index == at, own_row, row)
                column = jnp.where(index == at, own_column, column)
        return (
            rows_at(first_row + row, ROWS),
            pl.ds(pl.multiple_of(column, UNIT), width),
        )

    def width_of(s):
        return SLABS[s][2] if isinstance(s, int) else s[1]

    def index_of(s):
        return s if isinstance(s, int) else s[0]

    def of_own_width(condition, work):
        for width in WIDTHS:
            fits = jnp.where(x == 0, 768, jnp.where(x == XS // 2, 256, 512)) == width
            pl.when(condition & fits)(lambda width=width: work((x, width)))

    mine, other = core * HALF, (1 - core) * HALF
    def chunk_at(base, turn):
        return rows_at(base + turn * CHUNK, CHUNK)

    small_loads = [
        pltpu.make_async_copy(exp1_hbm, exp1, exp_sems.at[0]),
        pltpu.make_async_copy(exp2_hbm, exp2, exp_sems.at[1]),
    ]
    for copy in small_loads:
        copy.start()
    loads = {}
    for at, (base, turn) in enumerate(((other, 0), (other, 1), (mine, 0), (mine, 1))):
        rows = chunk_at(base, turn)
        for which, (source, target) in enumerate(((g_hbm.at[0], g), (f_hbm, f), (e_hbm.at[0], e))):
            copy = pltpu.make_async_copy(
                source.at[rows, :], target.at[rows, :], in_sems.at[3 * at + which]
            )
            copy.start()
            loads[at, which] = copy

    barrier = pltpu.get_barrier_semaphore()
    pl.semaphore_signal(barrier, inc=1, device_id={"rep": sibling}, device_id_type=MESH)

    def greet(at_core):
        @pl.loop(1, XS)
        def _(step):
            pl.semaphore_signal(
                barrier, inc=1, device_id=device(lax.rem(x + step, XS), 0, at_core),
                device_id_type=MESH,
            )

        @pl.loop(0, 2 * XS)
        def _(step):
            pl.semaphore_signal(
                barrier, inc=1, device_id=device(lax.rem(x + step // 2, XS), 1 + 2 * lax.rem(step, 2), at_core),
                device_id_type=MESH,
            )

    pl.when(owns)(lambda: greet(core))
    pl.when(owns_more)(lambda: greet(0))

    @pl.when(z == 1)
    def _():
        @pl.loop(0, XS)
        def _(step):
            pl.semaphore_signal(
                barrier, inc=1, device_id=device(lax.rem(x + step, XS), 2), device_id_type=MESH
            )

    matrix[...] = small_hadamard()
    for copy in small_loads:
        copy.wait()
    exponent1, exponent2 = columns_of(exp1[...], exp2[...])
    scale1 = power_two(exponent1)
    up1[...] = scale1
    down1[...] = power_two(-exponent1)

    def first(at, rows):
        for which in range(3):
            loads[at, which].wait()
        signs = f[rows, :].astype(jnp.float32)
        flipped = (g[rows, :].astype(jnp.float32) * signs).astype(jnp.bfloat16)
        rotated = rotate(flipped, matrix[...]) + e[rows, :]
        code = jnp.clip(rotated * wide(down1[rows, :], LENGTH), -448.0, 448.0).astype(jnp.bfloat16)
        err[rows, :] = rotated - code.astype(jnp.float32) * wide(up1[rows, :], LENGTH)
        codes[rows, :] = code

    to_sibling = []
    for chunk in range(2):
        first(chunk, chunk_at(other, chunk))
        if chunk == 0:
            pl.semaphore_wait(barrier, jnp.where(z == 0, XS, XS + 1))
        to_sibling.append(pltpu.make_async_remote_copy(
            src_ref=codes.at[chunk_at(other, chunk), :],
            dst_ref=from_sibling.at[chunk_at(0, chunk), :],
            send_sem=pair_send.at[chunk], recv_sem=pair_recv.at[chunk],
            device_id={"rep": sibling}, device_id_type=MESH,
        ))
        to_sibling[-1].start()
    for chunk in range(2):
        first(2 + chunk, chunk_at(mine, chunk))

    def to_owner(s):
        away = (elsewhere & (s == 0)).astype(jnp.int32)
        to_pass = z == 2
        buffer = jnp.where(to_pass, 0, away)
        pltpu.make_async_remote_copy(
            src_ref=sums.at[slab(s, 0)], dst_ref=parts.at[buffer, z, x, :, pl.ds(0, width_of(s))],
            send_sem=a_send, recv_sem=a_recv.at[buffer, z],
            device_id=device(s, jnp.where(to_pass, 1, 0), core + buffer), device_id_type=MESH,
        ).start()

    for chunk in range(2):
        to_sibling[chunk].wait()
        rows = chunk_at(0, chunk)
        pair = codes[chunk_at(mine, chunk), :].astype(jnp.float32)
        sums[rows, :] = (pair + from_sibling[rows, :].astype(jnp.float32)).astype(jnp.bfloat16)
        for turn in range(XS // 2):
            s = CHUNK_SLABS[chunk][turn]
            pl.when(jnp.logical_not(owns & (x == s)))(lambda s=s: to_owner(s))

    ratio[...] = scale1 * power_two(-exponent2)
    up2[...] = power_two(exponent2)

    def plane_sum(total, buffer, plane, count):
        for column in range(count):
            part = parts[buffer, plane, column, :, pl.ds(0, total.shape[1])]
            total = total + part.astype(jnp.float32)
        return total

    def slots(count, width):
        return parts.at[0, 0, pl.ds(0, count), :, pl.ds(0, width)]

    def wait_for(landed, sem):
        pltpu.make_async_copy(landed, landed, sem).wait()

    def pass_on(s):
        width = width_of(s)
        wait_for(slots(XS, width), a_recv.at[0, 2])
        total = plane_sum(jnp.zeros((ROWS, width), jnp.float32), 0, 2, XS)
        staged = passed.at[:, pl.ds(0, width)]
        staged[...] = total.astype(jnp.bfloat16)
        buffer = (elsewhere & (x == 0)).astype(jnp.int32)
        pltpu.make_async_remote_copy(
            src_ref=staged, dst_ref=parts.at[buffer, 2, 0, :, pl.ds(0, width)],
            send_sem=p_send, recv_sem=a_recv.at[buffer, 2],
            device_id=device(x, 0, core + buffer), device_id_type=MESH,
        ).start()

    of_own_width(z == 1, pass_on)

    def send_slab(s, at, device_id):
        own = slab(s, at)
        pltpu.make_async_remote_copy(
            src_ref=gathered.at[own], dst_ref=gathered.at[own],
            send_sem=x_send, recv_sem=x_recv.at[index_of(s)],
            device_id=device_id, device_id_type=MESH,
        ).start()

    def to_row(s):
        for px in EARLY_FIRST:
            pl.when(px != x)(lambda px=px: send_slab(s, mine, device(px, z)))

    def own_slab(s, buffer, at):
        own, width = slab(s, at), width_of(s)
        total = jnp.zeros((ROWS, width), jnp.float32)
        for plane in (0, 1, 3, 2):
            if plane == 0:
                wait_for(slots(XS - 1 + buffer, width), a_recv.at[buffer, 0])
            elif plane == 2:
                wait_for(slots(1, width), a_recv.at[buffer, 2])
            else:
                wait_for(slots(XS, width), a_recv.at[buffer, plane])
            total = plane_sum(total, buffer, plane, 1 if plane == 2 else XS)
        scaled = total * wide(ratio[own[0], :], width)
        gathered[own] = jnp.clip(scaled, -448.0, 448.0).astype(jnp.bfloat16)

    def wait_slab(s):
        own = slab(s, mine)
        wait_for(gathered.at[own], x_recv.at[index_of(s)])

    def to_other_core(s):
        own = slab(s, mine)
        pltpu.make_async_remote_copy(
            src_ref=gathered.at[own], dst_ref=gathered.at[own],
            send_sem=c_send, recv_sem=c_recv.at[index_of(s)],
            device_id={"rep": sibling}, device_id_type=MESH,
        ).start()

    def finish(s):
        parts[0, 0, x, :, pl.ds(0, width_of(s))] = sums[slab(s, 0)]
        own_slab(s, 0, mine)
        send_slab(s, mine, device(x, 1))
        to_row(s)
        send_slab(s, mine, device(x, 2))
        send_slab(s, mine, device(x, 3))

    of_own_width(owns, finish)

    @pl.when(owns_more)
    def _():
        own_slab(0, 1, 0)
        send_slab(0, 0, device(0, 1, 0))
        for px in EARLY_FIRST:
            send_slab(0, 0, device(px, 0, 0))
        send_slab(0, 0, device(0, 2, 0))
        send_slab(0, 0, device(0, 3, 0))

    def relay(s):
        wait_slab(s)
        to_row(s)

    of_own_width(z != 0, relay)

    def last(rows):
        restored = rotate(gathered[rows, :], matrix[...]) * wide(up2[rows, :], LENGTH)
        upd[rows, :] = restored * f[rows, :].astype(jnp.float32)

    def hand_over(order):
        for s in order:
            here = (s == x) & jnp.logical_not(late)
            pl.when(jnp.logical_not(here))(lambda s=s: wait_slab(s))
            if s == 0:
                pl.when(jnp.logical_not(late))(lambda: to_other_core(0))
            else:
                to_other_core(s)

    near_zero = (x < 3) | (x > 5)
    pl.when(near_zero)(lambda: hand_over((0, 1, 7, 2, 6, 3, 5, 4)))
    pl.when(jnp.logical_not(near_zero))(lambda: hand_over((4, 3, 5, 2, 6, 1, 7, 0)))
    last(rows_at(mine, HALF))
    for s in range(XS):
        if s == 0:
            pl.when(jnp.logical_not(owns_more))(lambda: wait_for(slots(1, width_of(0)), c_recv.at[0]))
        else:
            wait_for(slots(1, width_of(s)), c_recv.at[s])
    last(rows_at(other, HALF))

    def sent(units, sem):
        if units // 4:
            wait_for(codes.at[pl.ds(0, ROWS * (units // 4)), :], sem)
        if units % 4:
            wait_for(codes.at[pl.ds(0, ROWS), pl.ds(0, UNIT * (units % 4))], sem)

    def sent_all(s):
        units = width_of(s) // UNIT

        @pl.when(owns)
        def _():
            sent(4 * XS // 2 - units, a_send)
            sent(10 * units, x_send)

        @pl.when(z != 0)
        def _():
            sent((XS - 1) * units, x_send)

        @pl.when(z == 1)
        def _():
            sent(units, p_send)

    of_own_width(z >= 0, sent_all)
    pl.when(jnp.logical_not(owns))(lambda: sent(4 * XS // 2, a_send))
    pl.when(owns_more)(lambda: sent(11 * width_of(0) // UNIT, x_send))
    pl.when(jnp.logical_not(late))(lambda: sent(4 * XS // 2, c_send))
    pl.when(late)(lambda: sent(4 * XS // 2 - width_of(0) // UNIT, c_send))


def write_kernel(err, upd, err_hbm, upd_hbm, out_sems):
    stores = []
    for at in range(BLOCKS // CHUNK):
        rows = pl.ds(at * CHUNK, CHUNK)
        for which, (source, target) in enumerate(((err, err_hbm.at[0]), (upd, upd_hbm))):
            copy = pltpu.make_async_copy(
                source.at[rows, :], target.at[rows, :], out_sems.at[2 * at + which]
            )
            copy.start()
            stores.append(copy)
    for copy in stores:
        copy.wait()


def per_device(gradients, errors, sign_flips, first_exponents, second_exponents):
    hbm = pl.BlockSpec(memory_space=pl.ANY)
    vmem = pl.BlockSpec(memory_space=pltpu.VMEM)
    whole = (BLOCKS, LENGTH)
    f32, bf16, i32 = jnp.float32, jnp.bfloat16, jnp.int32
    dma = pltpu.SemaphoreType.DMA
    scale = pltpu.VMEM((BLOCKS, LANES), f32)
    arguments = (
        gradients, errors, sign_flips,
        first_exponents.reshape(1, BLOCKS), second_exponents.reshape(1, BLOCKS),
    )
    held = pl.pallas_call(
        reduce_kernel,
        out_shape=(pltpu.VMEM(whole, f32), pltpu.VMEM(whole, f32)),
        in_specs=[hbm] * 5,
        out_specs=(vmem, vmem),
        scratch_shapes=[
            pltpu.VMEM(whole, bf16), pltpu.VMEM(whole, f32), pltpu.VMEM(whole, i32),
            pltpu.VMEM(whole, bf16), pltpu.VMEM((HALF, LENGTH), bf16), pltpu.VMEM((HALF, LENGTH), bf16),
            pltpu.VMEM((2, ZS, XS, ROWS, COLS), bf16), pltpu.VMEM((ROWS, COLS), bf16),
            pltpu.VMEM(whole, bf16),
            pltpu.VMEM((FACTOR, FACTOR), bf16),
            pltpu.VMEM((1, BLOCKS), i32), pltpu.VMEM((1, BLOCKS), i32), scale, scale, scale, scale,
            dma((2,)), dma((12,)), dma((2,)), dma((2,)), dma, dma((2, ZS)), dma, dma, dma((XS,)),
            dma, dma((XS,)),
        ],
        compiler_params=pltpu.CompilerParams(
            collective_id=0, has_side_effects=True, vmem_limit_bytes=16 * 2**20
        ),
    )(*[pltpu.with_memory_space_constraint(array, pltpu.HBM) for array in arguments])
    return pl.pallas_call(
        write_kernel,
        out_shape=(jax.ShapeDtypeStruct((1, *whole), f32), jax.ShapeDtypeStruct(whole, f32)),
        in_specs=[vmem, vmem],
        out_specs=(hbm, hbm),
        scratch_shapes=[dma((2 * BLOCKS // CHUNK,))],
        compiler_params=pltpu.CompilerParams(vmem_limit_bytes=16 * 2**20),
    )(*held)


def solution(mesh):
    in_specs = (P("rep", "tp", None), P("rep", "tp", None), P("tp", None), P("tp"), P("tp"))
    out_specs = (P("rep", "tp", None), P("tp", None))
    return jax.shard_map(
        per_device, mesh=mesh, in_specs=in_specs, out_specs=out_specs, check_vma=False
    )
```

```python
import jax
import jax.numpy as jnp
from jax import lax
from jax.experimental import pallas as pl
from jax.experimental.pallas import tpu as pltpu
from jax.sharding import PartitionSpec as P

LENGTH = 1024
BLOCKS = 128
HALF = 64
XS = 8
ZS = 4
ROWS = 16
UNIT = 256
COLS = 768
LANES = 128
FACTOR = 256
PARTS = LENGTH // FACTOR
MESH = pl.DeviceIdType.MESH
CHUNK = 32
CHUNK_SLABS = ((0, 4, 3, 5), (1, 7, 2, 6))
SLABS = (
    (0, 0, 768), (48, 0, 512), (32, 0, 512), (16, 0, 512),
    (0, 768, 256), (16, 512, 512), (32, 512, 512), (48, 512, 512),
)
WIDTHS = (256, 512, 768)
EARLY_FIRST = (0, 1, 7, 2, 6, 3, 5, 4)
PAIRS = XS // 2


def small_hadamard():
    i = lax.broadcasted_iota(jnp.int32, (FACTOR, FACTOR), 0)
    j = lax.broadcasted_iota(jnp.int32, (FACTOR, FACTOR), 1)
    bits = i & j
    bits = bits ^ (bits >> 4)
    bits = bits ^ (bits >> 2)
    bits = bits ^ (bits >> 1)
    return jnp.where((bits & 1) == 1, -1.0 / 32.0, 1.0 / 32.0).astype(jnp.bfloat16)


def rotate(x, matrix):
    rows = x.shape[0]
    stacked = jnp.concatenate(
        [x[:, part * FACTOR : (part + 1) * FACTOR] for part in range(PARTS)], axis=0
    )
    product = jnp.dot(stacked, matrix, preferred_element_type=jnp.float32)
    a, b, c, d = [product[part * rows : (part + 1) * rows] for part in range(PARTS)]
    ab, amb, cd, cmd = a + b, a - b, c + d, c - d
    return jnp.concatenate([ab + cd, amb + cmd, ab - cd, amb - cmd], axis=1)


def columns_of(row1, row2):
    both = jnp.broadcast_to((row1 + 64 * row2).astype(jnp.float32), (BLOCKS, BLOCKS))
    i = lax.broadcasted_iota(jnp.int32, (BLOCKS, BLOCKS), 0)
    j = lax.broadcasted_iota(jnp.int32, (BLOCKS, BLOCKS), 1)
    column = jnp.sum(jnp.where(i == j, both, 0.0), axis=1, keepdims=True)
    packed = jnp.broadcast_to(column, (BLOCKS, LANES)).astype(jnp.int32)
    second = (packed + 32) >> 6
    return packed - 64 * second, second


def power_two(exponents):
    return (1 << (exponents + 16)).astype(jnp.float32) * jnp.float32(2.0**-16)


def wide(scale, columns):
    return jnp.concatenate([scale] * (columns // LANES), axis=1)


def reduce_kernel(
    g_hbm, e_hbm, f_hbm, exp1_hbm, exp2_hbm, err, upd,
    g, e, f, codes, from_sibling, sums, parts, passed, gathered, matrix, exp1, exp2, up1, down1, ratio, up2,
    exp_sems, in_sems, pair_send, pair_recv, a_send, a_recv, p_send, x_send, x_recv, c_send, c_recv,
):
    me = lax.axis_index("rep")
    core = lax.rem(me, 2)
    chip = me // 2
    x, z = chip // ZS, lax.rem(chip, ZS)
    sibling = me + 1 - 2 * core
    moved = lax.axis_index("tp") == 0
    late = moved & (x == 0) & (z == 0) & (core == 0)
    owns = (z == 0) & jnp.logical_not(late)
    owns_more = moved & (x == 0) & (z == 0) & (core == 1)
    elsewhere = moved & (core == 0)

    def device(px, pz, at_core=core):
        return {"rep": (px * ZS + pz) * 2 + at_core}

    def rows_at(first_row, count):
        return pl.ds(pl.multiple_of(first_row, ROWS), count)

    def slab(s, first_row):
        if isinstance(s, int):
            row, column, width = SLABS[s]
            return rows_at(first_row + row, ROWS), pl.ds(column, width)
        index, width = s
        row, column = jnp.int32(0), jnp.int32(0)
        for at, (own_row, own_column, own_width) in enumerate(SLABS):
            if own_width == width:
                row = jnp.where(index == at, own_row, row)
                column = jnp.where(index == at, own_column, column)
        return (
            rows_at(first_row + row, ROWS),
            pl.ds(pl.multiple_of(column, UNIT), width),
        )

    def width_of(s):
        return SLABS[s][2] if isinstance(s, int) else s[1]

    def index_of(s):
        return s if isinstance(s, int) else s[0]

    def of_own_width(condition, work):
        for width in WIDTHS:
            fits = jnp.where(x == 0, 768, jnp.where(x == XS // 2, 256, 512)) == width
            pl.when(condition & fits)(lambda width=width: work((x, width)))

    mine, other = core * HALF, (1 - core) * HALF
    def chunk_at(base, turn):
        return rows_at(base + turn * CHUNK, CHUNK)

    small_loads = [
        pltpu.make_async_copy(exp1_hbm, exp1, exp_sems.at[0]),
        pltpu.make_async_copy(exp2_hbm, exp2, exp_sems.at[1]),
    ]
    for copy in small_loads:
        copy.start()
    loads = {}
    for at, (base, turn) in enumerate(((other, 0), (other, 1), (mine, 0), (mine, 1))):
        rows = chunk_at(base, turn)
        for which, (source, target) in enumerate(((g_hbm.at[0], g), (f_hbm, f), (e_hbm.at[0], e))):
            copy = pltpu.make_async_copy(
                source.at[rows, :], target.at[rows, :], in_sems.at[3 * at + which]
            )
            copy.start()
            loads[at, which] = copy

    barrier = pltpu.get_barrier_semaphore()
    pl.semaphore_signal(barrier, inc=1, device_id={"rep": sibling}, device_id_type=MESH)

    def greet(at_core):
        @pl.loop(1, XS)
        def _(step):
            pl.semaphore_signal(
                barrier, inc=1, device_id=device(lax.rem(x + step, XS), 0, at_core),
                device_id_type=MESH,
            )

        @pl.loop(0, 2 * XS)
        def _(step):
            pl.semaphore_signal(
                barrier, inc=1, device_id=device(lax.rem(x + step // 2, XS), 1 + 2 * lax.rem(step, 2), at_core),
                device_id_type=MESH,
            )

    pl.when(owns)(lambda: greet(core))
    pl.when(owns_more)(lambda: greet(0))

    @pl.when(z == 1)
    def _():
        @pl.loop(0, XS)
        def _(step):
            pl.semaphore_signal(
                barrier, inc=1, device_id=device(lax.rem(x + step, XS), 2), device_id_type=MESH
            )

    matrix[...] = small_hadamard()
    for copy in small_loads:
        copy.wait()
    exponent1, exponent2 = columns_of(exp1[...], exp2[...])
    scale1 = power_two(exponent1)
    up1[...] = scale1
    down1[...] = power_two(-exponent1)

    def first(at, rows):
        for which in range(3):
            loads[at, which].wait()
        signs = f[rows, :].astype(jnp.float32)
        flipped = (g[rows, :].astype(jnp.float32) * signs).astype(jnp.bfloat16)
        rotated = rotate(flipped, matrix[...]) + e[rows, :]
        code = jnp.clip(rotated * wide(down1[rows, :], LENGTH), -448.0, 448.0).astype(jnp.bfloat16)
        err[rows, :] = rotated - code.astype(jnp.float32) * wide(up1[rows, :], LENGTH)
        codes[rows, :] = code

    to_sibling = []
    for chunk in range(2):
        first(chunk, chunk_at(other, chunk))
        if chunk == 0:
            pl.semaphore_wait(barrier, jnp.where(z == 0, XS, XS + 1))
        to_sibling.append(pltpu.make_async_remote_copy(
            src_ref=codes.at[chunk_at(other, chunk), :],
            dst_ref=from_sibling.at[chunk_at(0, chunk), :],
            send_sem=pair_send.at[chunk], recv_sem=pair_recv.at[chunk],
            device_id={"rep": sibling}, device_id_type=MESH,
        ))
        to_sibling[-1].start()
    for chunk in range(2):
        first(2 + chunk, chunk_at(mine, chunk))

    def to_owner(s):
        away = (elsewhere & (s == 0)).astype(jnp.int32)
        to_pass = z == 2
        buffer = jnp.where(to_pass, 0, away)
        pltpu.make_async_remote_copy(
            src_ref=sums.at[slab(s, 0)], dst_ref=parts.at[buffer, z, x, :, pl.ds(0, width_of(s))],
            send_sem=a_send, recv_sem=a_recv.at[buffer, z],
            device_id=device(s, jnp.where(to_pass, 1, 0), core + buffer), device_id_type=MESH,
        ).start()

    for chunk in range(2):
        to_sibling[chunk].wait()
        rows = chunk_at(0, chunk)
        pair = codes[chunk_at(mine, chunk), :].astype(jnp.float32)
        sums[rows, :] = (pair + from_sibling[rows, :].astype(jnp.float32)).astype(jnp.bfloat16)

        @pl.when(z != 0)
        def _():
            for s in CHUNK_SLABS[chunk]:
                to_owner(s)

        @pl.when(z == 0)
        def _():
            for s in CHUNK_SLABS[chunk]:
                pl.when(jnp.logical_not(owns & (x == s)))(lambda s=s: to_owner(s))

    ratio[...] = scale1 * power_two(-exponent2)
    up2[...] = power_two(exponent2)

    def plane_sum(total, buffer, plane, count):
        for column in range(count):
            part = parts[buffer, plane, column, :, pl.ds(0, total.shape[1])]
            total = total + part.astype(jnp.float32)
        return total

    def slots(count, width):
        return parts.at[0, 0, pl.ds(0, count), :, pl.ds(0, width)]

    def wait_for(landed, sem):
        pltpu.make_async_copy(landed, landed, sem).wait()

    def pass_on(s):
        width = width_of(s)
        wait_for(slots(XS, width), a_recv.at[0, 2])
        total = plane_sum(jnp.zeros((ROWS, width), jnp.float32), 0, 2, XS)
        staged = passed.at[:, pl.ds(0, width)]
        staged[...] = total.astype(jnp.bfloat16)
        buffer = (elsewhere & (x == 0)).astype(jnp.int32)
        pltpu.make_async_remote_copy(
            src_ref=staged, dst_ref=parts.at[buffer, 2, 0, :, pl.ds(0, width)],
            send_sem=p_send, recv_sem=a_recv.at[buffer, 2],
            device_id=device(x, 0, core + buffer), device_id_type=MESH,
        ).start()

    of_own_width(z == 1, pass_on)

    def send_slab(s, at, device_id):
        own = slab(s, at)
        pltpu.make_async_remote_copy(
            src_ref=gathered.at[own], dst_ref=gathered.at[own],
            send_sem=x_send, recv_sem=x_recv.at[index_of(s)],
            device_id=device_id, device_id_type=MESH,
        ).start()

    def to_row(s):
        reached = False
        for at in range(XS - 1):
            reached = (x == EARLY_FIRST[at]) | reached
            px = jnp.where(reached, EARLY_FIRST[at + 1], EARLY_FIRST[at])
            send_slab(s, mine, device(px, z))

    def own_slab(s, buffer, at):
        own, width = slab(s, at), width_of(s)
        total = jnp.zeros((ROWS, width), jnp.float32)
        for plane in (0, 1, 3, 2):
            if plane == 0:
                wait_for(slots(XS - 1 + buffer, width), a_recv.at[buffer, 0])
            elif plane == 2:
                wait_for(slots(1, width), a_recv.at[buffer, 2])
            else:
                wait_for(slots(XS, width), a_recv.at[buffer, plane])
            total = plane_sum(total, buffer, plane, 1 if plane == 2 else XS)
        scaled = total * wide(ratio[own[0], :], width)
        gathered[own] = jnp.clip(scaled, -448.0, 448.0).astype(jnp.bfloat16)

    def wait_slab(s):
        own = slab(s, mine)
        wait_for(gathered.at[own], x_recv.at[index_of(s)])

    def to_other_core(s):
        own = slab(s, mine)
        pltpu.make_async_remote_copy(
            src_ref=gathered.at[own], dst_ref=gathered.at[own],
            send_sem=c_send, recv_sem=c_recv.at[index_of(s)],
            device_id={"rep": sibling}, device_id_type=MESH,
        ).start()

    def finish(s):
        parts[0, 0, x, :, pl.ds(0, width_of(s))] = sums[slab(s, 0)]
        own_slab(s, 0, mine)
        send_slab(s, mine, device(x, 1))
        to_row(s)
        send_slab(s, mine, device(x, 2))
        send_slab(s, mine, device(x, 3))

    of_own_width(owns, finish)

    @pl.when(owns_more)
    def _():
        own_slab(0, 1, 0)
        send_slab(0, 0, device(0, 1, 0))
        for px in EARLY_FIRST:
            send_slab(0, 0, device(px, 0, 0))
        send_slab(0, 0, device(0, 2, 0))
        send_slab(0, 0, device(0, 3, 0))

    def relay(s):
        wait_slab(s)
        to_row(s)

    of_own_width(z != 0, relay)

    def last(rows):
        restored = rotate(gathered[rows, :], matrix[...]) * wide(up2[rows, :], LENGTH)
        upd[rows, :] = restored * f[rows, :].astype(jnp.float32)

    def hand_over(order):
        for s in order:
            here = (s == x) & jnp.logical_not(late)
            pl.when(jnp.logical_not(here))(lambda s=s: wait_slab(s))
            if s == 0:
                pl.when(jnp.logical_not(late))(lambda: to_other_core(0))
            else:
                to_other_core(s)

    near_zero = (x < 3) | (x > 5)
    pl.when(near_zero)(lambda: hand_over((0, 1, 7, 2, 6, 3, 5, 4)))
    pl.when(jnp.logical_not(near_zero))(lambda: hand_over((4, 3, 5, 2, 6, 1, 7, 0)))
    last(rows_at(mine, HALF))
    for s in range(XS):
        if s == 0:
            pl.when(jnp.logical_not(owns_more))(lambda: wait_for(slots(1, width_of(0)), c_recv.at[0]))
        else:
            wait_for(slots(1, width_of(s)), c_recv.at[s])
    last(rows_at(other, HALF))

    def sent(units, sem):
        if units // 4:
            wait_for(codes.at[pl.ds(0, ROWS * (units // 4)), :], sem)
        if units % 4:
            wait_for(codes.at[pl.ds(0, ROWS), pl.ds(0, UNIT * (units % 4))], sem)

    def sent_all(s):
        units = width_of(s) // UNIT

        @pl.when(owns)
        def _():
            sent(4 * XS // 2 - units, a_send)
            sent(10 * units, x_send)

        @pl.when(z != 0)
        def _():
            sent((XS - 1) * units, x_send)

        @pl.when(z == 1)
        def _():
            sent(units, p_send)

    of_own_width(z >= 0, sent_all)
    pl.when(jnp.logical_not(owns))(lambda: sent(4 * XS // 2, a_send))
    pl.when(owns_more)(lambda: sent(11 * width_of(0) // UNIT, x_send))
    pl.when(jnp.logical_not(late))(lambda: sent(4 * XS // 2, c_send))
    pl.when(late)(lambda: sent(4 * XS // 2 - width_of(0) // UNIT, c_send))


def write_kernel(err, upd, err_hbm, upd_hbm, out_sems):
    stores = []
    for at in range(BLOCKS // CHUNK):
        rows = pl.ds(at * CHUNK, CHUNK)
        for which, (source, target) in enumerate(((err, err_hbm.at[0]), (upd, upd_hbm))):
            copy = pltpu.make_async_copy(
                source.at[rows, :], target.at[rows, :], out_sems.at[2 * at + which]
            )
            copy.start()
            stores.append(copy)
    for copy in stores:
        copy.wait()


def per_device(gradients, errors, sign_flips, first_exponents, second_exponents):
    hbm = pl.BlockSpec(memory_space=pl.ANY)
    vmem = pl.BlockSpec(memory_space=pltpu.VMEM)
    whole = (BLOCKS, LENGTH)
    f32, bf16, i32 = jnp.float32, jnp.bfloat16, jnp.int32
    dma = pltpu.SemaphoreType.DMA
    scale = pltpu.VMEM((BLOCKS, LANES), f32)
    arguments = (
        gradients, errors, sign_flips,
        first_exponents.reshape(1, BLOCKS), second_exponents.reshape(1, BLOCKS),
    )
    held = pl.pallas_call(
        reduce_kernel,
        out_shape=(pltpu.VMEM(whole, f32), pltpu.VMEM(whole, f32)),
        in_specs=[hbm] * 5,
        out_specs=(vmem, vmem),
        scratch_shapes=[
            pltpu.VMEM(whole, bf16), pltpu.VMEM(whole, f32), pltpu.VMEM(whole, i32),
            pltpu.VMEM(whole, bf16), pltpu.VMEM((HALF, LENGTH), bf16), pltpu.VMEM((HALF, LENGTH), bf16),
            pltpu.VMEM((2, ZS, XS, ROWS, COLS), bf16), pltpu.VMEM((ROWS, COLS), bf16),
            pltpu.VMEM(whole, bf16),
            pltpu.VMEM((FACTOR, FACTOR), bf16),
            pltpu.VMEM((1, BLOCKS), i32), pltpu.VMEM((1, BLOCKS), i32), scale, scale, scale, scale,
            dma((2,)), dma((12,)), dma((2,)), dma((2,)), dma, dma((2, ZS)), dma, dma, dma((XS,)),
            dma, dma((XS,)),
        ],
        compiler_params=pltpu.CompilerParams(
            collective_id=0, has_side_effects=True, vmem_limit_bytes=16 * 2**20
        ),
    )(*[pltpu.with_memory_space_constraint(array, pltpu.HBM) for array in arguments])
    return pl.pallas_call(
        write_kernel,
        out_shape=(jax.ShapeDtypeStruct((1, *whole), f32), jax.ShapeDtypeStruct(whole, f32)),
        in_specs=[vmem, vmem],
        out_specs=(hbm, hbm),
        scratch_shapes=[dma((2 * BLOCKS // CHUNK,))],
        compiler_params=pltpu.CompilerParams(vmem_limit_bytes=16 * 2**20),
    )(*held)


def solution(mesh):
    in_specs = (P("rep", "tp", None), P("rep", "tp", None), P("tp", None), P("tp"), P("tp"))
    out_specs = (P("rep", "tp", None), P("tp", None))
    return jax.shard_map(
        per_device, mesh=mesh, in_specs=in_specs, out_specs=out_specs, check_vma=False
    )
```

```python
import jax
import jax.numpy as jnp
from jax import lax
from jax.experimental import pallas as pl
from jax.experimental.pallas import tpu as pltpu
from jax.sharding import PartitionSpec as P

LENGTH = 1024
BLOCKS = 128
HALF = 64
XS = 8
ZS = 4
ROWS = 16
UNIT = 256
COLS = 768
LANES = 128
FACTOR = 256
PARTS = LENGTH // FACTOR
MESH = pl.DeviceIdType.MESH
CHUNK = 64
CHUNKS = 1
CHUNK_SLABS = ((0, 1, 7, 4, 2, 6, 3, 5),)
SLABS = (
    (0, 0, 768), (48, 0, 512), (32, 0, 512), (16, 0, 512),
    (0, 768, 256), (16, 512, 512), (32, 512, 512), (48, 512, 512),
)
WIDTHS = (256, 512, 768)
EARLY_FIRST = (0, 1, 7, 2, 6, 3, 5, 4)
PAIRS = XS // 2


def small_hadamard():
    i = lax.broadcasted_iota(jnp.int32, (FACTOR, FACTOR), 0)
    j = lax.broadcasted_iota(jnp.int32, (FACTOR, FACTOR), 1)
    bits = i & j
    bits = bits ^ (bits >> 4)
    bits = bits ^ (bits >> 2)
    bits = bits ^ (bits >> 1)
    return jnp.where((bits & 1) == 1, -1.0 / 32.0, 1.0 / 32.0).astype(jnp.bfloat16)


def rotate(x, matrix):
    rows = x.shape[0]
    stacked = jnp.concatenate(
        [x[:, part * FACTOR : (part + 1) * FACTOR] for part in range(PARTS)], axis=0
    )
    product = jnp.dot(stacked, matrix, preferred_element_type=jnp.float32)
    a, b, c, d = [product[part * rows : (part + 1) * rows] for part in range(PARTS)]
    ab, amb, cd, cmd = a + b, a - b, c + d, c - d
    return jnp.concatenate([ab + cd, amb + cmd, ab - cd, amb - cmd], axis=1)


def columns_of(row1, row2):
    both = jnp.broadcast_to((row1 + 64 * row2).astype(jnp.float32), (BLOCKS, BLOCKS))
    i = lax.broadcasted_iota(jnp.int32, (BLOCKS, BLOCKS), 0)
    j = lax.broadcasted_iota(jnp.int32, (BLOCKS, BLOCKS), 1)
    column = jnp.sum(jnp.where(i == j, both, 0.0), axis=1, keepdims=True)
    packed = jnp.broadcast_to(column, (BLOCKS, LANES)).astype(jnp.int32)
    second = (packed + 32) >> 6
    return packed - 64 * second, second


def power_two(exponents):
    return (1 << (exponents + 16)).astype(jnp.float32) * jnp.float32(2.0**-16)


def wide(scale, columns):
    return jnp.concatenate([scale] * (columns // LANES), axis=1)


def reduce_kernel(
    g_hbm, e_hbm, f_hbm, exp1_hbm, exp2_hbm, err, upd,
    g, e, f, codes, from_sibling, sums, parts, passed, gathered, matrix, exp1, exp2, up1, down1, ratio, up2,
    exp_sems, in_sems, pair_send, pair_recv, a_send, a_recv, p_send, x_send, x_recv, c_send, c_recv,
):
    me = lax.axis_index("rep")
    core = lax.rem(me, 2)
    chip = me // 2
    x, z = chip // ZS, lax.rem(chip, ZS)
    sibling = me + 1 - 2 * core
    moved = lax.axis_index("tp") == 0
    late = moved & (x == 0) & (z == 0) & (core == 0)
    owns = (z == 0) & jnp.logical_not(late)
    owns_more = moved & (x == 0) & (z == 0) & (core == 1)
    elsewhere = moved & (core == 0)

    def device(px, pz, at_core=core):
        return {"rep": (px * ZS + pz) * 2 + at_core}

    def rows_at(first_row, count):
        return pl.ds(pl.multiple_of(first_row, ROWS), count)

    def slab(s, first_row):
        if isinstance(s, int):
            row, column, width = SLABS[s]
            return rows_at(first_row + row, ROWS), pl.ds(column, width)
        index, width = s
        row, column = jnp.int32(0), jnp.int32(0)
        for at, (own_row, own_column, own_width) in enumerate(SLABS):
            if own_width == width:
                row = jnp.where(index == at, own_row, row)
                column = jnp.where(index == at, own_column, column)
        return (
            rows_at(first_row + row, ROWS),
            pl.ds(pl.multiple_of(column, UNIT), width),
        )

    def width_of(s):
        return SLABS[s][2] if isinstance(s, int) else s[1]

    def index_of(s):
        return s if isinstance(s, int) else s[0]

    def of_own_width(condition, work):
        for width in WIDTHS:
            fits = jnp.where(x == 0, 768, jnp.where(x == XS // 2, 256, 512)) == width
            pl.when(condition & fits)(lambda width=width: work((x, width)))

    mine, other = core * HALF, (1 - core) * HALF
    def chunk_at(base, turn):
        return rows_at(base + turn * CHUNK, CHUNK)

    small_loads = [
        pltpu.make_async_copy(exp1_hbm, exp1, exp_sems.at[0]),
        pltpu.make_async_copy(exp2_hbm, exp2, exp_sems.at[1]),
    ]
    for copy in small_loads:
        copy.start()
    loads = {}
    places = [(base, turn) for base in (other, mine) for turn in range(CHUNKS)]
    for at, (base, turn) in enumerate(places):
        rows = chunk_at(base, turn)
        for which, (source, target) in enumerate(((g_hbm.at[0], g), (f_hbm, f), (e_hbm.at[0], e))):
            copy = pltpu.make_async_copy(
                source.at[rows, :], target.at[rows, :], in_sems.at[3 * at + which]
            )
            copy.start()
            loads[at, which] = copy

    barrier = pltpu.get_barrier_semaphore()
    pl.semaphore_signal(barrier, inc=1, device_id={"rep": sibling}, device_id_type=MESH)

    def greet(at_core):
        @pl.loop(1, XS)
        def _(step):
            pl.semaphore_signal(
                barrier, inc=1, device_id=device(lax.rem(x + step, XS), 0, at_core),
                device_id_type=MESH,
            )

        @pl.loop(0, 2 * XS)
        def _(step):
            pl.semaphore_signal(
                barrier, inc=1, device_id=device(lax.rem(x + step // 2, XS), 1 + 2 * lax.rem(step, 2), at_core),
                device_id_type=MESH,
            )

    pl.when(owns)(lambda: greet(core))
    pl.when(owns_more)(lambda: greet(0))

    @pl.when(z == 1)
    def _():
        @pl.loop(0, XS)
        def _(step):
            pl.semaphore_signal(
                barrier, inc=1, device_id=device(lax.rem(x + step, XS), 2), device_id_type=MESH
            )

    matrix[...] = small_hadamard()
    for copy in small_loads:
        copy.wait()
    exponent1, exponent2 = columns_of(exp1[...], exp2[...])
    scale1 = power_two(exponent1)
    up1[...] = scale1
    down1[...] = power_two(-exponent1)

    def first(at, rows):
        for which in range(3):
            loads[at, which].wait()
        signs = f[rows, :].astype(jnp.float32)
        flipped = (g[rows, :].astype(jnp.float32) * signs).astype(jnp.bfloat16)
        rotated = rotate(flipped, matrix[...]) + e[rows, :]
        code = jnp.clip(rotated * wide(down1[rows, :], LENGTH), -448.0, 448.0).astype(jnp.bfloat16)
        err[rows, :] = rotated - code.astype(jnp.float32) * wide(up1[rows, :], LENGTH)
        codes[rows, :] = code

    to_sibling = []
    for chunk in range(CHUNKS):
        first(chunk, chunk_at(other, chunk))
        if chunk == 0:
            pl.semaphore_wait(barrier, jnp.where(z == 0, XS, XS + 1))
        to_sibling.append(pltpu.make_async_remote_copy(
            src_ref=codes.at[chunk_at(other, chunk), :],
            dst_ref=from_sibling.at[chunk_at(0, chunk), :],
            send_sem=pair_send.at[chunk], recv_sem=pair_recv.at[chunk],
            device_id={"rep": sibling}, device_id_type=MESH,
        ))
        to_sibling[-1].start()
    for chunk in range(CHUNKS):
        first(CHUNKS + chunk, chunk_at(mine, chunk))

    def to_owner(s):
        away = (elsewhere & (s == 0)).astype(jnp.int32)
        to_pass = z == 2
        buffer = jnp.where(to_pass, 0, away)
        pltpu.make_async_remote_copy(
            src_ref=sums.at[slab(s, 0)], dst_ref=parts.at[buffer, z, x, :, pl.ds(0, width_of(s))],
            send_sem=a_send, recv_sem=a_recv.at[buffer, z],
            device_id=device(s, jnp.where(to_pass, 1, 0), core + buffer), device_id_type=MESH,
        ).start()

    for chunk in range(CHUNKS):
        to_sibling[chunk].wait()
        rows = chunk_at(0, chunk)
        pair = codes[chunk_at(mine, chunk), :].astype(jnp.float32)
        sums[rows, :] = (pair + from_sibling[rows, :].astype(jnp.float32)).astype(jnp.bfloat16)

        @pl.when(z != 0)
        def _():
            for s in CHUNK_SLABS[chunk]:
                to_owner(s)

        @pl.when(z == 0)
        def _():
            for s in CHUNK_SLABS[chunk]:
                pl.when(jnp.logical_not(owns & (x == s)))(lambda s=s: to_owner(s))

    ratio[...] = scale1 * power_two(-exponent2)
    up2[...] = power_two(exponent2)

    def plane_sum(total, buffer, plane, count):
        for column in range(count):
            part = parts[buffer, plane, column, :, pl.ds(0, total.shape[1])]
            total = total + part.astype(jnp.float32)
        return total

    def slots(count, width):
        return parts.at[0, 0, pl.ds(0, count), :, pl.ds(0, width)]

    def wait_for(landed, sem):
        pltpu.make_async_copy(landed, landed, sem).wait()

    def pass_on(s):
        width = width_of(s)
        wait_for(slots(XS, width), a_recv.at[0, 2])
        total = plane_sum(jnp.zeros((ROWS, width), jnp.float32), 0, 2, XS)
        staged = passed.at[:, pl.ds(0, width)]
        staged[...] = total.astype(jnp.bfloat16)
        buffer = (elsewhere & (x == 0)).astype(jnp.int32)
        pltpu.make_async_remote_copy(
            src_ref=staged, dst_ref=parts.at[buffer, 2, 0, :, pl.ds(0, width)],
            send_sem=p_send, recv_sem=a_recv.at[buffer, 2],
            device_id=device(x, 0, core + buffer), device_id_type=MESH,
        ).start()

    of_own_width(z == 1, pass_on)

    def send_slab(s, at, device_id):
        own = slab(s, at)
        pltpu.make_async_remote_copy(
            src_ref=gathered.at[own], dst_ref=gathered.at[own],
            send_sem=x_send, recv_sem=x_recv.at[index_of(s)],
            device_id=device_id, device_id_type=MESH,
        ).start()

    def to_row(s):
        reached = False
        for at in range(XS - 1):
            reached = (x == EARLY_FIRST[at]) | reached
            px = jnp.where(reached, EARLY_FIRST[at + 1], EARLY_FIRST[at])
            send_slab(s, mine, device(px, z))

    def own_slab(s, buffer, at):
        own, width = slab(s, at), width_of(s)
        total = jnp.zeros((ROWS, width), jnp.float32)
        for plane in (0, 1, 3, 2):
            if plane == 0:
                wait_for(slots(XS - 1 + buffer, width), a_recv.at[buffer, 0])
            elif plane == 2:
                wait_for(slots(1, width), a_recv.at[buffer, 2])
            else:
                wait_for(slots(XS, width), a_recv.at[buffer, plane])
            total = plane_sum(total, buffer, plane, 1 if plane == 2 else XS)
        scaled = total * wide(ratio[own[0], :], width)
        gathered[own] = jnp.clip(scaled, -448.0, 448.0).astype(jnp.bfloat16)

    def wait_slab(s):
        own = slab(s, mine)
        wait_for(gathered.at[own], x_recv.at[index_of(s)])

    def to_other_core(s):
        own = slab(s, mine)
        pltpu.make_async_remote_copy(
            src_ref=gathered.at[own], dst_ref=gathered.at[own],
            send_sem=c_send, recv_sem=c_recv.at[index_of(s)],
            device_id={"rep": sibling}, device_id_type=MESH,
        ).start()

    def finish(s):
        parts[0, 0, x, :, pl.ds(0, width_of(s))] = sums[slab(s, 0)]
        own_slab(s, 0, mine)
        send_slab(s, mine, device(x, 1))
        to_row(s)
        send_slab(s, mine, device(x, 2))
        send_slab(s, mine, device(x, 3))

    of_own_width(owns, finish)

    @pl.when(owns_more)
    def _():
        own_slab(0, 1, 0)
        send_slab(0, 0, device(0, 1, 0))
        for px in EARLY_FIRST:
            send_slab(0, 0, device(px, 0, 0))
        send_slab(0, 0, device(0, 2, 0))
        send_slab(0, 0, device(0, 3, 0))

    def relay(s):
        wait_slab(s)
        to_row(s)

    of_own_width(z != 0, relay)

    def last(rows):
        restored = rotate(gathered[rows, :], matrix[...]) * wide(up2[rows, :], LENGTH)
        upd[rows, :] = restored * f[rows, :].astype(jnp.float32)

    def hand_over(order):
        for s in order:
            here = (s == x) & jnp.logical_not(late)
            pl.when(jnp.logical_not(here))(lambda s=s: wait_slab(s))
            if s == 0:
                pl.when(jnp.logical_not(late))(lambda: to_other_core(0))
            else:
                to_other_core(s)

    near_zero = (x < 3) | (x > 5)
    pl.when(near_zero)(lambda: hand_over((0, 1, 7, 2, 6, 3, 5, 4)))
    pl.when(jnp.logical_not(near_zero))(lambda: hand_over((4, 3, 5, 2, 6, 1, 7, 0)))
    last(rows_at(mine, HALF))
    for s in range(XS):
        if s == 0:
            pl.when(jnp.logical_not(owns_more))(lambda: wait_for(slots(1, width_of(0)), c_recv.at[0]))
        else:
            wait_for(slots(1, width_of(s)), c_recv.at[s])
    last(rows_at(other, HALF))

    def sent(units, sem):
        if units // 4:
            wait_for(codes.at[pl.ds(0, ROWS * (units // 4)), :], sem)
        if units % 4:
            wait_for(codes.at[pl.ds(0, ROWS), pl.ds(0, UNIT * (units % 4))], sem)

    def sent_all(s):
        units = width_of(s) // UNIT

        @pl.when(owns)
        def _():
            sent(4 * XS // 2 - units, a_send)
            sent(10 * units, x_send)

        @pl.when(z != 0)
        def _():
            sent((XS - 1) * units, x_send)

        @pl.when(z == 1)
        def _():
            sent(units, p_send)

    of_own_width(z >= 0, sent_all)
    pl.when(jnp.logical_not(owns))(lambda: sent(4 * XS // 2, a_send))
    pl.when(owns_more)(lambda: sent(11 * width_of(0) // UNIT, x_send))
    pl.when(jnp.logical_not(late))(lambda: sent(4 * XS // 2, c_send))
    pl.when(late)(lambda: sent(4 * XS // 2 - width_of(0) // UNIT, c_send))


def write_kernel(err, upd, err_hbm, upd_hbm, out_sems):
    stores = []
    for at in range(BLOCKS // 32):
        rows = pl.ds(at * 32, 32)
        for which, (source, target) in enumerate(((err, err_hbm.at[0]), (upd, upd_hbm))):
            copy = pltpu.make_async_copy(
                source.at[rows, :], target.at[rows, :], out_sems.at[2 * at + which]
            )
            copy.start()
            stores.append(copy)
    for copy in stores:
        copy.wait()


def per_device(gradients, errors, sign_flips, first_exponents, second_exponents):
    hbm = pl.BlockSpec(memory_space=pl.ANY)
    vmem = pl.BlockSpec(memory_space=pltpu.VMEM)
    whole = (BLOCKS, LENGTH)
    f32, bf16, i32 = jnp.float32, jnp.bfloat16, jnp.int32
    dma = pltpu.SemaphoreType.DMA
    scale = pltpu.VMEM((BLOCKS, LANES), f32)
    arguments = (
        gradients, errors, sign_flips,
        first_exponents.reshape(1, BLOCKS), second_exponents.reshape(1, BLOCKS),
    )
    held = pl.pallas_call(
        reduce_kernel,
        out_shape=(pltpu.VMEM(whole, f32), pltpu.VMEM(whole, f32)),
        in_specs=[hbm] * 5,
        out_specs=(vmem, vmem),
        scratch_shapes=[
            pltpu.VMEM(whole, bf16), pltpu.VMEM(whole, f32), pltpu.VMEM(whole, i32),
            pltpu.VMEM(whole, bf16), pltpu.VMEM((HALF, LENGTH), bf16), pltpu.VMEM((HALF, LENGTH), bf16),
            pltpu.VMEM((2, ZS, XS, ROWS, COLS), bf16), pltpu.VMEM((ROWS, COLS), bf16),
            pltpu.VMEM(whole, bf16),
            pltpu.VMEM((FACTOR, FACTOR), bf16),
            pltpu.VMEM((1, BLOCKS), i32), pltpu.VMEM((1, BLOCKS), i32), scale, scale, scale, scale,
            dma((2,)), dma((6 * CHUNKS,)), dma((CHUNKS,)), dma((CHUNKS,)), dma, dma((2, ZS)), dma, dma, dma((XS,)),
            dma, dma((XS,)),
        ],
        compiler_params=pltpu.CompilerParams(
            collective_id=0, has_side_effects=True, vmem_limit_bytes=16 * 2**20
        ),
    )(*[pltpu.with_memory_space_constraint(array, pltpu.HBM) for array in arguments])
    return pl.pallas_call(
        write_kernel,
        out_shape=(jax.ShapeDtypeStruct((1, *whole), f32), jax.ShapeDtypeStruct(whole, f32)),
        in_specs=[vmem, vmem],
        out_specs=(hbm, hbm),
        scratch_shapes=[dma((2 * BLOCKS // 32,))],
        compiler_params=pltpu.CompilerParams(vmem_limit_bytes=16 * 2**20),
    )(*held)


def solution(mesh):
    in_specs = (P("rep", "tp", None), P("rep", "tp", None), P("tp", None), P("tp"), P("tp"))
    out_specs = (P("rep", "tp", None), P("tp", None))
    return jax.shard_map(
        per_device, mesh=mesh, in_specs=in_specs, out_specs=out_specs, check_vma=False
    )
```
